32 devices in a mesh: lat: 4 (over x, core), lon: 8 (over z, y).
Axes of the slice: x: 2, y: 2, z: 4, core: 2. Of those that a mesh axis runs over, the one named last changes fastest.
Arguments:
- tokens: bfloat16 [2, 24, 96, 192], P(None, 'lat', 'lon'), may hold values from -6 to 6
- gain_one: float32 [192], replicated, may hold values from 0.1 to 1.9
- gain_two: float32 [192], replicated, may hold values from 0.1 to 1.9
- qkv_weight: bfloat16 [192, 576], replicated, may hold values from -0.4375 to 0.4375
- proj_weight: bfloat16 [192, 192], replicated, may hold values from -0.4375 to 0.4375
- up_weight: bfloat16 [192, 768], replicated, may hold values from -0.4375 to 0.4375
- down_weight: bfloat16 [768, 192], replicated, may hold values from -0.21875 to 0.21875
- bias_table: float32 [6, 1, 4, 3312], P(None, None, 'lat'), may hold values from -6 to 306
- pos_index: int32 [144, 144], replicated, may hold values from 0 to 3311
- mask_ids: int32 [2, 24, 96], P(None, 'lat', 'lon'), may hold values from 0 to 2
- cotangent: bfloat16 [2, 24, 96, 192], P(None, 'lat', 'lon'), may hold values from -6 to 6
Outputs:
- output: bfloat16 [2, 24, 96, 192], P(None, 'lat', 'lon')
- delta_tokens: bfloat16 [2, 24, 96, 192], P(None, 'lat', 'lon')
- grad_gain_one: float32 [192], replicated
- grad_gain_two: float32 [192], replicated
- grad_qkv: float32 [192, 576], replicated
- grad_proj: float32 [192, 192], replicated
- grad_up: float32 [192, 768], replicated
- grad_down: float32 [768, 192], replicated
- grad_bias: float32 [6, 1, 4, 3312], P(None, None, 'lat')
The draws below stay inside these ranges and needn't reach their ends.
All inputs are finite; a program needn't handle non-finite values.
Results may differ from the reference program's by a relative error of at most 0.025.
Values may be sent and summed in bfloat16 or wider, within the bound.
A program may use at most 64 MiB of HBM per device.

```python
import jax
import jax.numpy as jnp
from jax import lax

C = 192
HEADS = 6
HID = 768
WZ = 2
WLAT = 6
WLON = 12
WT = 144
NPOS = 3312
Z = 2
NLAT = 24
NLON = 96
NZW = 1
NLW = 4
TOKENS = 4608


def draw_bias_table(key, part):
    key = jax.random.fold_in(key, 11)
    first = jax.random.fold_in(key, 0)
    shape = (HEADS, NZW, NLW, NPOS)
    base = jnp.clip(jax.random.normal(first, shape, jnp.float32), -6.0, 6.0)
    return base


def set_ends(result, stream_key, least, high):
    shape = result.shape
    spot = [jax.random.randint(jax.random.fold_in(stream_key, axis), (), 0, shape[axis]) for axis in range(len(shape))]
    result = result.at[tuple(spot)].set(least)
    longest = shape.index(max(shape))
    spot[longest] = (spot[longest] + 1) % shape[longest]
    return result.at[tuple(spot)].set(high)


def steps_of(stream_key, shape, cuts, smallest, largest):
    def one(axis_at, blocks):
        heights = jax.random.uniform(jax.random.fold_in(jax.random.fold_in(stream_key, 6), axis_at), (blocks,), jnp.float32, smallest / len(cuts), largest / len(cuts))
        return jnp.repeat(jnp.exp(heights), shape[axis_at] // blocks).reshape((-1,) + (1,) * (len(shape) - axis_at - 1))

    level = one(*cuts[0])
    for cut in cuts[1:]:
        level = level * one(*cut)
    return level


def gaussian(key, extent, scale, reach, cuts=(), dtype=jnp.bfloat16):
    drawn = scale * jax.random.normal(key, extent, jnp.float32)
    if cuts:
        drawn = drawn * steps_of(key, extent, cuts, -0.22, 0.18)
    return jnp.clip(drawn, -reach, reach).astype(dtype)


def setup_inputs(seed: int = 0) -> dict:
    streams_of = jax.random.split(jax.random.key(seed), 12)
    tokens = gaussian(streams_of[0], (Z, NLAT, NLON, C), 1.0, 6.0, ((1, 4), (2, 8)))
    gain_one = jnp.clip(1.0 + 0.18 * jax.random.normal(streams_of[1], (C,), jnp.float32), 0.1, 1.9)
    gain_two = jnp.clip(1.0 + 0.18 * jax.random.normal(streams_of[2], (C,), jnp.float32), 0.1, 1.9)
    qkv_weight = gaussian(streams_of[3], (C, 3 * C), C ** -0.5, 0.4375)
    proj_weight = gaussian(streams_of[4], (C, C), C ** -0.5, 0.4375)
    up_weight = gaussian(streams_of[5], (C, HID), C ** -0.5, 0.4375)
    down_weight = gaussian(streams_of[6], (HID, C), HID ** -0.5, 0.21875)
    bias_table = draw_bias_table(jax.random.fold_in(streams_of[11], 71), 0)
    pos_index = set_ends(jax.random.randint(streams_of[8], (WT, WT), 0, NPOS), jax.random.fold_in(streams_of[8], 1), 0, NPOS - 1).astype(jnp.int32)
    mask_ids = set_ends(jax.random.randint(streams_of[9], (Z, NLAT, NLON), 0, 3), jax.random.fold_in(streams_of[9], 1), 0, 2).astype(jnp.int32)
    cotangent = gaussian(streams_of[10], (Z, NLAT, NLON, C), 1.0, 6.0, ((1, 4), (2, 8)))
    return {"tokens": tokens, "gain_one": gain_one, "gain_two": gain_two, "qkv_weight": qkv_weight, "proj_weight": proj_weight, "up_weight": up_weight, "down_weight": down_weight, "bias_table": bias_table, "pos_index": pos_index, "mask_ids": mask_ids, "cotangent": cotangent}


EPS = 1e-05

def norm_stats(values):
    widened = values.astype(jnp.float32)
    center = widened - lax.optimization_barrier(jnp.mean(widened, axis=-1, keepdims=True))
    spread = lax.optimization_barrier(jnp.mean(center * center, axis=-1, keepdims=True))
    inverse = lax.rsqrt(spread + EPS)
    return (center * inverse, inverse)

def norm_back(delta_hidden, normal, inverse, gain):
    grad_gain = lax.optimization_barrier(jnp.sum((delta_hidden * normal).reshape(-1, normal.shape[-1]), axis=0))
    delta_normal = delta_hidden * gain
    delta_input = inverse * (delta_normal - lax.optimization_barrier(jnp.mean(delta_normal, axis=-1, keepdims=True)) - normal * lax.optimization_barrier(jnp.mean(delta_normal * normal, axis=-1, keepdims=True)))
    return (delta_input, grad_gain)

def gelu_pair(up_proj):
    cumulative = 0.5 * (1.0 + lax.erf(up_proj * 0.7071067811865476))
    density = jnp.exp(-0.5 * up_proj * up_proj) * 0.3989422804014327
    return (up_proj * cumulative, cumulative + up_proj * density)

def mlp_block(middle, gain_two, up_weight, down_weight, cotangent):
    normal, inverse = norm_stats(middle)
    normed = (normal * gain_two).astype(jnp.bfloat16)
    up_proj = jnp.dot(normed, up_weight, preferred_element_type=jnp.float32)
    active, slope = gelu_pair(up_proj)
    active = active.astype(jnp.bfloat16)
    output = (middle.astype(jnp.float32) + jnp.dot(active, down_weight, preferred_element_type=jnp.float32)).astype(jnp.bfloat16)
    grad_down = jnp.dot(active.T, cotangent, preferred_element_type=jnp.float32)
    delta_act = jnp.dot(cotangent, down_weight.T, preferred_element_type=jnp.float32)
    delta_up = (delta_act * slope).astype(jnp.bfloat16)
    grad_up = jnp.dot(normed.T, delta_up, preferred_element_type=jnp.float32)
    delta_hidden = jnp.dot(delta_up, up_weight.T, preferred_element_type=jnp.float32)
    delta_input, grad_gain = norm_back(delta_hidden, normal, inverse, gain_two)
    delta_middle = (cotangent.astype(jnp.float32) + delta_input).astype(jnp.bfloat16)
    return (output, delta_middle, grad_gain, grad_up, grad_down)

def to_windows(layout):
    levels, lat_rows, lon_cols, features = layout.shape
    layout = layout.reshape(levels // WZ, WZ, lat_rows // WLAT, WLAT, lon_cols // WLON, WLON, features)
    layout = layout.transpose(2, 0, 4, 1, 3, 5, 6)
    return layout.reshape(lat_rows // WLAT, levels // WZ, lon_cols // WLON, WZ * WLAT * WLON, features)

def from_windows(windows, levels, lat_rows, lon_cols):
    features = windows.shape[-1]
    windows = windows.reshape(lat_rows // WLAT, levels // WZ, lon_cols // WLON, WZ, WLAT, WLON, features)
    windows = windows.transpose(1, 3, 0, 4, 2, 5, 6)
    return windows.reshape(levels, lat_rows, lon_cols, features)

def bias_pairs(bias_table, pos_index):
    head_count, level_blocks, lat_blocks = bias_table.shape[:3]
    picked = jnp.take(bias_table, pos_index.reshape(-1), axis=3)
    picked = picked.reshape(head_count, level_blocks, lat_blocks, WT, WT).transpose(2, 1, 0, 3, 4)
    return picked[:, :, None]

def table_grad(delta_type, pos_index):
    lat_blocks, level_blocks, head_count = delta_type.shape[:3]
    flattened = delta_type.reshape(lat_blocks, level_blocks, head_count, WT * WT).transpose(3, 2, 1, 0)
    summed = jax.ops.segment_sum(flattened, pos_index.reshape(-1), num_segments=NPOS)
    return summed.transpose(1, 2, 3, 0)

def attend(windows, mask_win, bias_win, qkv_weight):
    leading = windows.shape[:-2]
    features = windows.shape[-1]
    head_size = features // HEADS
    packed = jnp.dot(windows.reshape(-1, features), qkv_weight, preferred_element_type=jnp.float32)
    packed = lax.optimization_barrier(packed.astype(jnp.bfloat16))
    packed = packed.reshape(leading + (WT, 3, HEADS, head_size))
    queries = packed[..., 0, :, :]
    key_heads = packed[..., 1, :, :]
    values = packed[..., 2, :, :]
    factor = head_size ** (-0.5)
    scores = jnp.einsum('...phd,...rhd->...hpr', queries.astype(jnp.float32), key_heads.astype(jnp.float32)) * factor + bias_win
    allowed = mask_win[..., None, :, None] == mask_win[..., None, None, :]
    scores = jnp.where(allowed, scores, -1e+30)
    row_top = lax.optimization_barrier(jnp.max(scores, axis=-1, keepdims=True))
    weight = jnp.exp(scores - row_top)
    attn_prob = weight / lax.optimization_barrier(jnp.sum(weight, axis=-1, keepdims=True))
    rounded = lax.optimization_barrier(attn_prob.astype(jnp.bfloat16))
    mixture = jnp.einsum('...hpr,...rhd->...phd', rounded.astype(jnp.float32), values.astype(jnp.float32)).astype(jnp.bfloat16)
    return (mixture.reshape(leading + (WT, features)), (queries, key_heads, values, attn_prob, rounded))

def attend_back(windows, qkv_weight, stored, delta_mixture):
    queries, key_heads, values, attn_prob, rounded = stored
    leading = windows.shape[:-2]
    features = windows.shape[-1]
    head_size = features // HEADS
    factor = head_size ** (-0.5)
    delta_heads = delta_mixture.reshape(leading + (WT, HEADS, head_size)).astype(jnp.float32)
    delta_probs = jnp.einsum('...phd,...rhd->...hpr', delta_heads, values.astype(jnp.float32))
    delta_values = jnp.einsum('...hpr,...phd->...rhd', rounded.astype(jnp.float32), delta_heads)
    delta_scores = attn_prob * (delta_probs - lax.optimization_barrier(jnp.sum(delta_probs * attn_prob, axis=-1, keepdims=True)))
    delta_low = lax.optimization_barrier(delta_scores.astype(jnp.bfloat16)).astype(jnp.float32)
    delta_query = jnp.einsum('...hpr,...rhd->...phd', delta_low, key_heads.astype(jnp.float32)) * factor
    delta_keys = jnp.einsum('...hpr,...phd->...rhd', delta_low, queries.astype(jnp.float32)) * factor
    delta_packed = jnp.stack((delta_query, delta_keys, delta_values), axis=-3).astype(jnp.bfloat16).reshape(-1, 3 * features)
    flattened = windows.reshape(-1, features)
    grad_qkv = jnp.dot(flattened.T, delta_packed, preferred_element_type=jnp.float32)
    delta_window = jnp.dot(delta_packed, qkv_weight.T, preferred_element_type=jnp.float32).astype(jnp.bfloat16)
    return (delta_window.reshape(leading + (WT, features)), grad_qkv, delta_scores)

def reference(tokens, gain_one, gain_two, qkv_weight, proj_weight, up_weight, down_weight, bias_table, pos_index, mask_ids, cotangent):
    levels, lat_rows, lon_cols, features = tokens.shape
    backward_shift = (-1, -(WLAT // 2), -(WLON // 2))
    forward_shift = (1, WLAT // 2, WLON // 2)
    normal_one, inverse_one = norm_stats(tokens)
    normed = (normal_one * gain_one).astype(jnp.bfloat16)
    windows = to_windows(jnp.roll(normed, backward_shift, (0, 1, 2)))
    mask_win = to_windows(mask_ids[..., None])[..., 0]
    bias_win = bias_pairs(bias_table, pos_index)

    def forward_row(member):
        mixture_row, stored = attend(member[0], member[1], member[2], qkv_weight)
        return mixture_row
    mixture = lax.map(forward_row, (windows, mask_win, bias_win))
    flat_mix = mixture.reshape(-1, features)
    attn_win = jnp.dot(flat_mix, proj_weight, preferred_element_type=jnp.float32).astype(jnp.bfloat16)
    attention = jnp.roll(from_windows(attn_win.reshape(mixture.shape), levels, lat_rows, lon_cols), forward_shift, (0, 1, 2))
    middle = (tokens.astype(jnp.float32) + attention.astype(jnp.float32)).astype(jnp.bfloat16)

    def mlp_level(member):
        return mlp_block(member[0].reshape(-1, features), gain_two, up_weight, down_weight, member[1].reshape(-1, features))
    output, delta_middle, gain_parts, up_parts, down_parts = lax.map(mlp_level, (middle, cotangent))
    output = output.reshape(tokens.shape)
    delta_middle = delta_middle.reshape(tokens.shape)
    grad_gain_two = lax.optimization_barrier(jnp.sum(gain_parts, axis=0))
    grad_up = lax.optimization_barrier(jnp.sum(up_parts, axis=0))
    grad_down = lax.optimization_barrier(jnp.sum(down_parts, axis=0))
    delta_attn = to_windows(jnp.roll(delta_middle, backward_shift, (0, 1, 2)))
    flat_delta = delta_attn.reshape(-1, features)
    grad_proj = jnp.dot(flat_mix.T, flat_delta, preferred_element_type=jnp.float32)
    delta_mixture = jnp.dot(flat_delta, proj_weight.T, preferred_element_type=jnp.float32).astype(jnp.bfloat16).reshape(mixture.shape)

    def backward_row(member):
        mixture_row, stored = attend(member[0], member[1], member[2], qkv_weight)
        delta_window, grad_part, delta_scores = attend_back(member[0], qkv_weight, stored, member[3])
        return (delta_window, grad_part, lax.optimization_barrier(jnp.sum(delta_scores, axis=1)))
    delta_window, qkv_parts, delta_type = lax.map(backward_row, (windows, mask_win, bias_win, delta_mixture))
    grad_qkv = lax.optimization_barrier(jnp.sum(qkv_parts, axis=0))
    grad_bias = table_grad(delta_type, pos_index)
    delta_normed = jnp.roll(from_windows(delta_window, levels, lat_rows, lon_cols), forward_shift, (0, 1, 2))
    delta_input, grad_gain_one = norm_back(delta_normed.astype(jnp.float32), normal_one, inverse_one, gain_one)
    delta_tokens = (delta_middle.astype(jnp.float32) + delta_input).astype(jnp.bfloat16)
    factor = TOKENS ** (-0.5)
    return (output, delta_tokens, grad_gain_one * factor, grad_gain_two * factor, grad_qkv * factor, grad_proj * factor, grad_up * factor, grad_down * factor, grad_bias)
```

```python
import functools
import math

import jax
import jax.numpy as jnp
import numpy as np
from jax import lax
from jax.experimental import pallas as pl
from jax.experimental.pallas import tpu as pltpu
from jax.sharding import PartitionSpec as P

HEADS = 6
WZ = 2
WLAT = 6
WLON = 12
WT = 144
NPOS = 3312
C = 192
HID = 768
HD = 32
SLOT = 48
NT = 4 * SLOT
LANES = 128
HI = 32
HI_USED = -(-NPOS // LANES)
EPS = 1e-05
F32 = jnp.float32
BF16 = jnp.bfloat16
MESH = pl.DeviceIdType.MESH


def orders():
    grid = np.zeros((NT, WT), np.float32)
    window = np.zeros((256, WT), np.float32)
    for rh in range(2):
        for ch in range(2):
            for z in range(2):
                for r in range(3):
                    for c in range(6):
                        row = (rh * 2 + ch) * SLOT + z * 18 + r * 6 + c
                        grid[row, z * 72 + (3 * rh + r) * 12 + 6 * ch + c] = 1
                        window[row, (1 - z) * 72 + (3 * (1 - rh) + r) * 12 + 6 * (1 - ch) + c] = 1
    return grid, window


def mm(a, b):
    return lax.dot_general(a, b, (((1,), (0,)), ((), ())), preferred_element_type=F32)


def mm_nt(a, b):
    return lax.dot_general(a, b, (((1,), (1,)), ((), ())), preferred_element_type=F32)


def mm_tn(a, b):
    return lax.dot_general(a, b, (((0,), (0,)), ((), ())), preferred_element_type=F32)


def norm_stats(widened):
    center = widened - jnp.mean(widened, axis=-1, keepdims=True)
    spread = jnp.mean(center * center, axis=-1, keepdims=True)
    inverse = lax.rsqrt(spread + EPS)
    return center * inverse, inverse


def norm_back(delta_hidden, normal, inverse, gain):
    grad_gain = jnp.sum(delta_hidden * normal, axis=0, keepdims=True)
    delta_normal = delta_hidden * gain
    delta_input = inverse * (
        delta_normal
        - jnp.mean(delta_normal, axis=-1, keepdims=True)
        - normal * jnp.mean(delta_normal * normal, axis=-1, keepdims=True)
    )
    return delta_input, grad_gain


class Exchange:
    def __init__(self, place, axis, send_sem, recv_sem):
        self.lat, self.lon, self.n_lat, self.n_lon = place
        self.axis = axis
        self.n = self.n_lat if axis == 0 else self.n_lon
        self.me = self.lat if axis == 0 else self.lon
        self.send_sem, self.recv_sem = send_sem, recv_sem
        self.copies = []

    def peer(self, d):
        to = lax.rem(self.me + d, self.n)
        return to, ((to, self.lon) if self.axis == 0 else (self.lat, to))

    def start(self, d, src, dst, device):
        copy = pltpu.make_async_remote_copy(
            src_ref=src,
            dst_ref=dst,
            send_sem=self.send_sem.at[d - 1],
            recv_sem=self.recv_sem.at[d - 1],
            device_id=device,
            device_id_type=MESH,
        )
        copy.start()
        self.copies.append(copy)

    def scatter(self, src, got, rows):
        self.src, self.got, self.rows = src, got, rows
        for d in range(1, self.n):
            to, device = self.peer(d)
            piece = pl.ds(pl.multiple_of(to * rows, 16), rows)
            self.start(d, src.at[piece], got.at[pl.ds((d - 1) * rows, rows)], device)

    def gather(self, whole, rows, start):
        piece = pl.ds(start, rows)
        for d in range(1, self.n):
            _, device = self.peer(d)
            self.start(d, whole.at[piece], whole.at[piece], device)

    def wait(self):
        for copy in self.copies:
            copy.wait()

    def total(self):
        self.wait()
        rows = self.rows
        own = pl.ds(pl.multiple_of(self.me * rows, 16), rows)
        out = self.src[own, :].astype(F32)
        for d in range(1, self.n):
            out = out + self.got[pl.ds((d - 1) * rows, rows), :].astype(F32)
        return out


def kernel(
    n_lat,
    n_lon,
    factor,
    rp1,
    rp2,
    rpb,
    tokens_ref,
    cot_ref,
    gain1_ref,
    gain2_ref,
    wqkv_ref,
    wproj_ref,
    wup_ref,
    wdown_ref,
    table_ref,
    pos_ref,
    mask_ref,
    grid_ref,
    win_ref,
    out_ref,
    dtok_ref,
    ggain_ref,
    gqkv_ref,
    gproj_ref,
    gup_ref,
    gdown_ref,
    gbias_ref,
    xs,
    xr,
    hi_ref,
    lo_ref,
    bias_ref,
    prob_ref,
    ds_ref,
    mix_ref,
    dpk_ref,
    pack_ref,
    gains_ref,
    buf1,
    got1,
    mid1,
    gom1,
    all1,
    buf2,
    got2,
    mid2,
    gom2,
    all2,
    bufb,
    gotb,
    allb,
    x_send,
    x_recv,
    lat_send,
    lat_recv,
    lon_send,
    lon_recv,
):
    lat, lon = lax.axis_index("lat"), lax.axis_index("lon")
    place = (lat, lon, n_lat, n_lon)
    next_lat, next_lon = lax.rem(lat + 1, n_lat), lax.rem(lon + 1, n_lon)
    prev_lat, prev_lon = lax.rem(lat + n_lat - 1, n_lat), lax.rem(lon + n_lon - 1, n_lon)
    befores = ((prev_lat, prev_lon), (prev_lat, lon), (lat, prev_lon))
    afters = ((next_lat, next_lon), (next_lat, lon), (lat, next_lon))

    barrier = pltpu.get_barrier_semaphore()
    peers = [(lax.rem(lat + d, n_lat), lon) for d in range(1, n_lat)]
    peers += [(lat, lax.rem(lon + d, n_lon)) for d in range(1, n_lon)]
    peers += [befores[0], afters[0]]
    for peer in peers:
        pl.semaphore_signal(barrier, inc=1, device_id=peer, device_id_type=MESH)

    def send_slots(e, devices):
        copies = []
        for s in range(3):
            piece = pl.ds(s * SLOT, SLOT)
            copy = pltpu.make_async_remote_copy(
                src_ref=xs.at[e, piece],
                dst_ref=xr.at[e, piece],
                send_sem=x_send.at[e, s],
                recv_sem=x_recv.at[e, s],
                device_id=devices[s],
                device_id_type=MESH,
            )
            copy.start()
            copies.append(copy)
        xr[e, 3 * SLOT :, :] = xs[e, 3 * SLOT :, :]
        return copies

    def finish(copies):
        for copy in copies:
            copy.wait()

    grid = grid_ref[...]
    tokens = mm(grid, tokens_ref[...])
    normal_one, inverse_one = norm_stats(tokens)
    gain_one = gain1_ref[...]
    xs[0] = (normal_one * gain_one).astype(BF16)
    pl.semaphore_wait(barrier, len(peers))
    copies = send_slots(0, befores)

    win = win_ref[...]
    win_rows = win[:NT]
    pos = pos_ref[...]
    hi = (pos >> 7).astype(F32).astype(BF16)
    lo = (pos & 127).astype(F32).astype(BF16)
    hi_ref[...] = mm_nt(mm(win_rows, hi).astype(BF16), win).astype(jnp.int32)
    lo_ref[...] = mm_nt(mm(win_rows, lo).astype(BF16), win).astype(jnp.int32)
    mask = jnp.broadcast_to((mask_ref[...] + 1).astype(F32), (8, WT)).astype(BF16)
    mask_row = mm_nt(mask, win)[0:1, :]
    mask_col = mm_nt(win_rows, mask)[:, 0:1]
    prob_ref[0] = jnp.where(mask_col == mask_row, 0.0, -1e30)

    step = 16

    def pick(block, carry):
        rows = pl.ds(pl.multiple_of(block * step, step), step)
        for half in range(2):
            cols = pl.ds(half * LANES, LANES)
            hi_here, lo_here = hi_ref[rows, cols], lo_ref[rows, cols]
            drop = prob_ref[0, rows, cols]
            acc = [drop] * HEADS
            for k in range(HI_USED):
                here = hi_here == k
                for h in range(HEADS):
                    row = jnp.broadcast_to(table_ref[pl.ds(h * HI + k, 1), :], (step, LANES))
                    got = jnp.take_along_axis(row, lo_here, axis=1, mode="promise_in_bounds")
                    acc[h] = jnp.where(here, got + drop, acc[h])
            for h in range(HEADS):
                bias_ref[h, rows, cols] = acc[h]
        return carry

    lax.fori_loop(0, NT // step, pick, 0)

    finish(copies)
    windows = xr[0]
    packed = mm(windows, wqkv_ref[...]).astype(BF16)
    scale = HD**-0.5

    def head(h, part):
        return packed[:, part * C + h * HD : part * C + (h + 1) * HD]

    for h in range(HEADS):
        scores = mm_nt(head(h, 0), head(h, 1)) * scale + bias_ref[h, :, :NT]
        weight = jnp.exp(scores - jnp.max(scores, axis=-1, keepdims=True))
        prob = weight / jnp.sum(weight, axis=-1, keepdims=True)
        prob_ref[h, :, :NT] = prob
        mix_ref[:, h * HD : (h + 1) * HD] = mm(prob.astype(BF16), head(h, 2))
    mixture = mix_ref[...].astype(BF16)
    xs[1] = mm(mixture, wproj_ref[...]).astype(BF16)
    copies = send_slots(1, afters)

    cot = mm(grid, cot_ref[...]).astype(BF16)
    delta_act = mm_nt(cot, wdown_ref[...])
    buf1[2304:, :] = jnp.zeros((buf1.shape[0] - 2304, LANES), BF16)
    buf2[1152:, :] = jnp.zeros((buf2.shape[0] - 1152, LANES), BF16)
    bufb[...] = jnp.zeros(bufb.shape, BF16)
    ds_ref[...] = jnp.zeros(ds_ref.shape, F32)
    gains_ref[...] = jnp.zeros(gains_ref.shape, F32)
    finish(copies)

    middle = (tokens + xr[1].astype(F32)).astype(BF16).astype(F32)
    normal_two, inverse_two = norm_stats(middle)
    gain_two = gain2_ref[...]
    normed_two = (normal_two * gain_two).astype(BF16)
    up = mm(normed_two, wup_ref[...])
    cumulative = 0.5 * (1.0 + lax.erf(up * 0.7071067811865476))
    density = jnp.exp(-0.5 * up * up) * 0.3989422804014327
    active = (up * cumulative).astype(BF16)
    delta_up = (delta_act * (cumulative + up * density)).astype(BF16)
    delta_hidden = mm_nt(delta_up, wup_ref[...])
    delta_input, grad_gain_two = norm_back(delta_hidden, normal_two, inverse_two, gain_two)
    delta_middle = (cot.astype(F32) + delta_input).astype(BF16)
    xs[2] = delta_middle
    copies = send_slots(2, befores)

    grad_up = mm_tn(normed_two, delta_up).astype(BF16)
    for j in range(6):
        buf1[j * C : (j + 1) * C, :] = grad_up[:, j * LANES : (j + 1) * LANES]
    grad_down = mm_tn(active, cot)
    buf1[1152:1920, :] = grad_down[:, :LANES].astype(BF16)
    pack_ref[:HID // 2, :64] = grad_down[: HID // 2, LANES:]
    pack_ref[:HID // 2, 64:128] = grad_down[HID // 2 :, LANES:]
    buf1[1920:2304, :] = pack_ref[: HID // 2, :LANES].astype(BF16)

    def exchange(axis, k):
        if axis == 0:
            return Exchange(place, 0, lat_send.at[k], lat_recv.at[k])
        return Exchange(place, 1, lon_send.at[k], lon_recv.at[k])

    rq1, rq2 = rp1 * n_lon, rp2 * n_lon
    scatter_lat1 = exchange(0, 0)
    scatter_lat1.scatter(buf1, got1, rq1)
    output = middle + mm(active, wdown_ref[...])
    out_ref[...] = mm_tn(grid, output.astype(BF16)).astype(BF16)
    finish(copies)

    delta_attn = xr[2]
    delta_mix = mm_nt(delta_attn, wproj_ref[...]).astype(BF16)
    pack_ref[:C, 3 * C :] = mm_tn(mixture, delta_attn)
    for h in range(HEADS):
        cols = slice(h * HD, (h + 1) * HD)
        delta_head = delta_mix[:, cols]
        prob = prob_ref[h, :, :NT]
        delta_prob = mm_nt(delta_head, head(h, 2))
        scored = prob * (delta_prob - jnp.sum(delta_prob * prob, axis=-1, keepdims=True))
        ds_ref[h, :, :NT] = scored
        low = scored.astype(BF16)
        dpk_ref[:, h * HD : (h + 1) * HD] = mm(low, head(h, 1)) * scale
        dpk_ref[:, C + h * HD : C + (h + 1) * HD] = mm_tn(low, head(h, 0)) * scale
        dpk_ref[:, 2 * C + h * HD : 2 * C + (h + 1) * HD] = mm_tn(prob.astype(BF16), delta_head)
    delta_packed = dpk_ref[...].astype(BF16)
    xs[3] = mm_nt(delta_packed, wqkv_ref[...]).astype(BF16)
    copies = send_slots(3, afters)

    mid1[...] = scatter_lat1.total().astype(BF16)
    scatter_lon1 = exchange(1, 0)
    scatter_lon1.scatter(mid1, gom1, rp1)
    pack_ref[:C, : 3 * C] = mm_tn(windows, delta_packed)
    for j in range(6):
        buf2[j * C : (j + 1) * C, :] = pack_ref[:C, j * LANES : (j + 1) * LANES].astype(BF16)
    finish(copies)

    delta_normed = xr[3].astype(F32)
    delta_input, grad_gain_one = norm_back(delta_normed, normal_one, inverse_one, gain_one)
    gains_ref[0:1, :C] = grad_gain_one
    gains_ref[1:2, :C] = grad_gain_two
    buf2[1152:1168, :] = gains_ref[:, :LANES].astype(BF16)
    buf2[1168:1184, :] = gains_ref[:, LANES:].astype(BF16)
    scatter_lat2 = exchange(0, 1)
    scatter_lat2.scatter(buf2, got2, rq2)
    delta_tokens = (delta_middle.astype(F32) + delta_input).astype(BF16)
    dtok_ref[...] = mm_tn(grid, delta_tokens).astype(BF16)

    def own_rows(rows):
        return pl.multiple_of((lat * n_lon + lon) * rows, 16)

    start1 = own_rows(rp1)
    all1[pl.ds(start1, rp1), :] = (scatter_lon1.total() * factor).astype(BF16)
    gather_lon1 = exchange(1, 1)
    gather_lon1.gather(all1, rp1, start1)

    iota_hi = lax.broadcasted_iota(jnp.int32, (HI, 256), 0)
    iota_lo = lax.broadcasted_iota(jnp.int32, (LANES, 256), 0)

    def collect(block, acc):
        slot = block // 5
        rows = pl.ds(pl.multiple_of(slot * SLOT + (block - slot * 5) * 8, 8), 8)
        hi_rows, lo_rows = hi_ref[rows, :], lo_ref[rows, :]
        ds_rows = [ds_ref[h, rows, :] for h in range(HEADS)]
        left, right = [], []
        for i in range(8):
            here = iota_hi == hi_rows[i : i + 1, :]
            left.append(
                jnp.concatenate(
                    [jnp.where(here, rows_h[i : i + 1, :], 0.0).astype(BF16) for rows_h in ds_rows],
                    axis=0,
                )
            )
            right.append(
                jnp.where(iota_lo == lo_rows[i : i + 1, :], 1.0, 0.0).astype(BF16)
            )
        return acc + mm_nt(jnp.concatenate(left, axis=1), jnp.concatenate(right, axis=1))

    bias_sum = lax.fori_loop(0, 20, collect, jnp.zeros((HEADS * HI, LANES), F32))
    bufb[: HEADS * HI, :] = bias_sum.astype(BF16)
    scatter_b = exchange(1, 2)
    scatter_b.scatter(bufb, gotb, rpb)

    mid2[...] = scatter_lat2.total().astype(BF16)
    scatter_lon2 = exchange(1, 3)
    scatter_lon2.scatter(mid2, gom2, rp2)

    gather_lon1.wait()
    gather_lat1 = exchange(0, 2)
    gather_lat1.gather(all1, rq1, pl.multiple_of(lat * rq1, 16))

    startb = pl.multiple_of(lon * rpb, 16)
    allb[pl.ds(startb, rpb), :] = scatter_b.total().astype(BF16)
    gather_b = exchange(1, 4)
    gather_b.gather(allb, rpb, startb)

    start2 = own_rows(rp2)
    all2[pl.ds(start2, rp2), :] = (scatter_lon2.total() * factor).astype(BF16)
    gather_lon2 = exchange(1, 5)
    gather_lon2.gather(all2, rp2, start2)
    gather_lon2.wait()
    gather_lat2 = exchange(0, 3)
    gather_lat2.gather(all2, rq2, pl.multiple_of(lat * rq2, 16))

    gather_b.wait()
    gbias_ref[...] = allb[: HEADS * HI, :].astype(F32)
    gather_lat1.wait()
    for j in range(6):
        gup_ref[:, j * LANES : (j + 1) * LANES] = all1[j * C : (j + 1) * C, :].astype(F32)
    gdown_ref[:, :LANES] = all1[1152:1920, :].astype(F32)
    tail = all1[1920:2304, :].astype(F32)
    gdown_ref[: HID // 2, LANES:] = tail[:, :64]
    gdown_ref[HID // 2 :, LANES:] = tail[:, 64:]
    gather_lat2.wait()
    for j in range(6):
        pack_ref[:C, j * LANES : (j + 1) * LANES] = all2[j * C : (j + 1) * C, :].astype(F32)
    gqkv_ref[...] = pack_ref[:C, : 3 * C]
    gproj_ref[...] = pack_ref[:C, 3 * C :]
    ggain_ref[:, :LANES] = all2[1152:1168, :].astype(F32)
    ggain_ref[:, LANES:] = all2[1168:1184, :].astype(F32)


def up_to(value, unit):
    return -(-value // unit) * unit


def local(
    n_lat,
    n_lon,
    tokens,
    gain_one,
    gain_two,
    qkv_weight,
    proj_weight,
    up_weight,
    down_weight,
    bias_table,
    pos_index,
    mask_ids,
    cotangent,
):
    n = n_lat * n_lon
    factor = 1.0 / math.sqrt(WT * n)
    rp1 = up_to(-(-2304 // n), 16)
    rp2 = up_to(-(-1184 // n), 16)
    rpb = up_to(-(-HEADS * HI // n_lon), 16)
    grid, window = orders()
    table = jnp.pad(bias_table.reshape(HEADS, NPOS), ((0, 0), (0, HI * LANES - NPOS)))
    args = (
        tokens.reshape(WT, C),
        cotangent.reshape(WT, C),
        gain_one.reshape(1, C),
        gain_two.reshape(1, C),
        qkv_weight,
        proj_weight,
        up_weight,
        down_weight,
        table.reshape(HEADS * HI, LANES),
        pos_index,
        mask_ids.reshape(1, WT),
        jnp.asarray(grid, BF16),
        jnp.asarray(window, BF16),
    )
    shape = jax.ShapeDtypeStruct
    outs = (
        shape((WT, C), BF16),
        shape((WT, C), BF16),
        shape((16, 256), F32),
        shape((C, 3 * C), F32),
        shape((C, C), F32),
        shape((C, HID), F32),
        shape((HID, C), F32),
        shape((HEADS * HI, LANES), F32),
    )

    def rows(count):
        return pltpu.VMEM((count, LANES), BF16)

    dma = pltpu.SemaphoreType.DMA
    scratch = [
        pltpu.VMEM((4, NT, C), BF16),
        pltpu.VMEM((4, NT, C), BF16),
        pltpu.VMEM((NT, 256), jnp.int32),
        pltpu.VMEM((NT, 256), jnp.int32),
        pltpu.VMEM((HEADS, NT, 256), F32),
        pltpu.VMEM((HEADS, NT, 256), F32),
        pltpu.VMEM((HEADS, NT, 256), F32),
        pltpu.VMEM((NT, C), F32),
        pltpu.VMEM((NT, 3 * C), F32),
        pltpu.VMEM((HID // 2, HID), F32),
        pltpu.VMEM((16, 256), F32),
    ]
    for rp in (rp1, rp2):
        scratch += [
            rows(rp * n),
            rows(rp * n_lon * (n_lat - 1)),
            rows(rp * n_lon),
            rows(rp * (n_lon - 1)),
            rows(rp * n),
        ]
    scratch += [rows(rpb * n_lon), rows(rpb * (n_lon - 1)), rows(rpb * n_lon)]
    scratch += [
        dma((4, 3)),
        dma((4, 3)),
        dma((4, n_lat - 1)),
        dma((4, n_lat - 1)),
        dma((6, n_lon - 1)),
        dma((6, n_lon - 1)),
    ]
    vmem = pl.BlockSpec(memory_space=pltpu.VMEM)
    out, dtok, ggain, gqkv, gproj, gup, gdown, gbias = pl.pallas_call(
        functools.partial(kernel, n_lat, n_lon, factor, rp1, rp2, rpb),
        out_shape=outs,
        in_specs=[vmem] * len(args),
        out_specs=[vmem] * len(outs),
        scratch_shapes=scratch,
        compiler_params=pltpu.CompilerParams(
            collective_id=0, has_side_effects=True, vmem_limit_bytes=48 * 1024 * 1024
        ),
    )(*args)
    return (
        out.reshape(tokens.shape),
        dtok.reshape(tokens.shape),
        ggain[0, :C],
        ggain[1, :C],
        gqkv,
        gproj,
        gup,
        gdown,
        gbias.reshape(HEADS, HI * LANES)[:, :NPOS].reshape(bias_table.shape),
    )


def solution(mesh):
    grid = P(None, "lat", "lon", None)
    table = P(None, None, "lat", None)
    in_specs = (grid, P(), P(), P(), P(), P(), P(), table, P(), P(None, "lat", "lon"), grid)
    out_specs = (grid, grid, P(), P(), P(), P(), P(), P(), table)
    body = functools.partial(local, mesh.shape["lat"], mesh.shape["lon"])
    return jax.shard_map(
        body, mesh=mesh, in_specs=in_specs, out_specs=out_specs, check_vma=False
    )
```

```python
import functools
import math

import jax
import jax.numpy as jnp
import numpy as np
from jax import lax
from jax.experimental import pallas as pl
from jax.experimental.pallas import tpu as pltpu
from jax.sharding import PartitionSpec as P

HEADS = 6
WZ = 2
WLAT = 6
WLON = 12
WT = 144
NPOS = 3312
C = 192
HID = 768
HD = 32
SLOT = 48
NT = 4 * SLOT
LANES = 128
HI = 32
HI_USED = -(-NPOS // LANES)
EPS = 1e-05
F32 = jnp.float32
BF16 = jnp.bfloat16
MESH = pl.DeviceIdType.MESH


def orders():
    grid = np.zeros((NT, WT), np.float32)
    window = np.zeros((256, WT), np.float32)
    for rh in range(2):
        for ch in range(2):
            for z in range(2):
                for r in range(3):
                    for c in range(6):
                        row = (rh * 2 + ch) * SLOT + z * 18 + r * 6 + c
                        grid[row, z * 72 + (3 * rh + r) * 12 + 6 * ch + c] = 1
                        window[row, (1 - z) * 72 + (3 * (1 - rh) + r) * 12 + 6 * (1 - ch) + c] = 1
    return grid, window


def mm(a, b):
    return lax.dot_general(a, b, (((1,), (0,)), ((), ())), preferred_element_type=F32)


def mm_nt(a, b):
    return lax.dot_general(a, b, (((1,), (1,)), ((), ())), preferred_element_type=F32)


def mm_tn(a, b):
    return lax.dot_general(a, b, (((0,), (0,)), ((), ())), preferred_element_type=F32)


def norm_stats(widened):
    center = widened - jnp.mean(widened, axis=-1, keepdims=True)
    spread = jnp.mean(center * center, axis=-1, keepdims=True)
    inverse = lax.rsqrt(spread + EPS)
    return center * inverse, inverse


def norm_back(delta_hidden, normal, inverse, gain):
    grad_gain = jnp.sum(delta_hidden * normal, axis=0, keepdims=True)
    delta_normal = delta_hidden * gain
    delta_input = inverse * (
        delta_normal
        - jnp.mean(delta_normal, axis=-1, keepdims=True)
        - normal * jnp.mean(delta_normal * normal, axis=-1, keepdims=True)
    )
    return delta_input, grad_gain


class Exchange:
    def __init__(self, place, axis, send_sem, recv_sem):
        self.lat, self.lon, self.n_lat, self.n_lon = place
        self.axis = axis
        self.n = self.n_lat if axis == 0 else self.n_lon
        self.me = self.lat if axis == 0 else self.lon
        self.send_sem, self.recv_sem = send_sem, recv_sem
        self.copies = []

    def peer(self, d):
        to = lax.rem(self.me + d, self.n)
        return to, ((to, self.lon) if self.axis == 0 else (self.lat, to))

    def start(self, d, src, dst, device):
        copy = pltpu.make_async_remote_copy(
            src_ref=src,
            dst_ref=dst,
            send_sem=self.send_sem.at[d - 1],
            recv_sem=self.recv_sem.at[d - 1],
            device_id=device,
            device_id_type=MESH,
        )
        copy.start()
        self.copies.append(copy)

    def scatter(self, src, got, rows):
        self.src, self.got, self.rows = src, got, rows
        for d in range(1, self.n):
            to, device = self.peer(d)
            piece = pl.ds(pl.multiple_of(to * rows, 16), rows)
            self.start(d, src.at[piece], got.at[pl.ds((d - 1) * rows, rows)], device)

    def gather(self, whole, rows, start):
        piece = pl.ds(start, rows)
        for d in range(1, self.n):
            _, device = self.peer(d)
            self.start(d, whole.at[piece], whole.at[piece], device)

    def wait(self):
        for copy in self.copies:
            copy.wait()

    def total(self):
        self.wait()
        rows = self.rows
        own = pl.ds(pl.multiple_of(self.me * rows, 16), rows)
        out = self.src[own, :].astype(F32)
        for d in range(1, self.n):
            out = out + self.got[pl.ds((d - 1) * rows, rows), :].astype(F32)
        return out


def kernel(
    n_lat,
    n_lon,
    factor,
    rp1,
    rp2,
    rpb,
    tokens_ref,
    cot_ref,
    gain1_ref,
    gain2_ref,
    wqkv_in,
    wproj_in,
    wup_in,
    wdown_in,
    table_in,
    pos_in,
    mask_ref,
    grid_ref,
    win_in,
    out_ref,
    dtok_ref,
    ggain_ref,
    all1,
    all2,
    allb,
    wqkv_ref,
    wproj_ref,
    wup_ref,
    wdown_ref,
    pos_ref,
    win_ref,
    load_sem,
    table_ref,
    xs,
    xr,
    hi_ref,
    lo_ref,
    bias_ref,
    prob_ref,
    ds_ref,
    pack_ref,
    gains_lat,
    gains_lon,
    buf1,
    got1,
    mid1,
    gom1,
    buf2,
    got2,
    mid2,
    gom2,
    bufb,
    gotb,
    x_send,
    x_recv,
    lat_send,
    lat_recv,
    lon_send,
    lon_recv,
):
    lat, lon = lax.axis_index("lat"), lax.axis_index("lon")
    place = (lat, lon, n_lat, n_lon)
    next_lat, next_lon = lax.rem(lat + 1, n_lat), lax.rem(lon + 1, n_lon)
    prev_lat, prev_lon = lax.rem(lat + n_lat - 1, n_lat), lax.rem(lon + n_lon - 1, n_lon)
    befores = ((prev_lat, prev_lon), (prev_lat, lon), (lat, prev_lon))
    afters = ((next_lat, next_lon), (next_lat, lon), (lat, next_lon))

    barrier = pltpu.get_barrier_semaphore()
    peers = [(lax.rem(lat + d, n_lat), lon) for d in range(1, n_lat)]
    peers += [(lat, lax.rem(lon + d, n_lon)) for d in range(1, n_lon)]
    peers += [befores[0], afters[0]]
    for peer in peers:
        pl.semaphore_signal(barrier, inc=1, device_id=peer, device_id_type=MESH)

    loads = {}
    for k, (name, src, dst) in enumerate(
        (
            ("pos", pos_in, pos_ref),
            ("win", win_in, win_ref),
            ("qkv", wqkv_in, wqkv_ref),
            ("proj", wproj_in, wproj_ref),
            ("down", wdown_in, wdown_ref),
            ("up", wup_in, wup_ref),
        )
    ):
        loads[name] = pltpu.make_async_copy(src, dst, load_sem.at[k])
        loads[name].start()

    def send_slots(e, devices):
        copies = []
        for s in range(3):
            piece = pl.ds(s * SLOT, SLOT)
            copy = pltpu.make_async_remote_copy(
                src_ref=xs.at[e, piece],
                dst_ref=xr.at[e, piece],
                send_sem=x_send.at[e, s],
                recv_sem=x_recv.at[e, s],
                device_id=devices[s],
                device_id_type=MESH,
            )
            copy.start()
            copies.append(copy)
        xr[e, 3 * SLOT :, :] = xs[e, 3 * SLOT :, :]
        return copies

    def finish(copies):
        for copy in copies:
            copy.wait()

    grid = grid_ref[...]
    tokens = mm(grid, tokens_ref[...])
    normal_one, inverse_one = norm_stats(tokens)
    gain_one = gain1_ref[...]
    xs[0] = (normal_one * gain_one).astype(BF16)
    pl.semaphore_wait(barrier, len(peers))
    copies = send_slots(0, befores)

    loads["pos"].wait()
    loads["win"].wait()
    for h in range(HEADS):
        for k in range(HI_USED):
            wide = min(LANES, NPOS - k * LANES)
            row = pl.ds(h * HI + k, 1)
            table_ref[row, :wide] = table_in[h, :, k * LANES : k * LANES + wide]
        if NPOS % LANES:
            table_ref[h * HI + HI_USED - 1 : h * HI + HI_USED, NPOS % LANES :] = jnp.zeros(
                (1, LANES - NPOS % LANES), F32
            )
    win = win_ref[...]
    win_rows = win[:NT]
    pos = pos_ref[...]
    hi = (pos >> 7).astype(F32).astype(BF16)
    lo = (pos & 127).astype(F32).astype(BF16)
    hi_ref[...] = mm_nt(mm(win_rows, hi).astype(BF16), win).astype(jnp.int32)
    lo_ref[...] = mm_nt(mm(win_rows, lo).astype(BF16), win).astype(jnp.int32)
    mask = jnp.broadcast_to((mask_ref[...] + 1).astype(F32), (8, WT)).astype(BF16)
    mask_row = mm_nt(mask, win)[0:1, :]
    mask_col = mm_nt(win_rows, mask)[:, 0:1]
    prob_ref[0] = jnp.where(mask_col == mask_row, 0.0, -1e30)

    step = 16

    def pick(block, carry):
        rows = pl.ds(pl.multiple_of(block * step, step), step)
        for half in range(2):
            cols = pl.ds(half * LANES, LANES)
            hi_here, lo_here = hi_ref[rows, cols], lo_ref[rows, cols]
            drop = prob_ref[0, rows, cols]
            acc = [drop] * HEADS
            for k in range(HI_USED):
                here = hi_here == k
                for h in range(HEADS):
                    row = jnp.broadcast_to(table_ref[pl.ds(h * HI + k, 1), :], (step, LANES))
                    got = jnp.take_along_axis(row, lo_here, axis=1, mode="promise_in_bounds")
                    acc[h] = jnp.where(here, got + drop, acc[h])
            for h in range(HEADS):
                bias_ref[h, rows, cols] = acc[h]
        return carry

    lax.fori_loop(0, NT // step, pick, 0)

    finish(copies)
    windows = xr[0]
    loads["qkv"].wait()
    packed = mm(windows, wqkv_ref[...]).astype(BF16)
    query, key, value = (packed[:, part * C : (part + 1) * C] for part in range(3))
    scale = HD**-0.5
    lane_head = lax.broadcasted_iota(jnp.int32, (1, C), 1) // HD
    picks = [jnp.where(lane_head == h, 1.0, 0.0).astype(BF16) for h in range(HEADS)]

    mixed = jnp.zeros((NT, C), F32)
    for h in range(HEADS):
        scores = mm_nt(query * picks[h], key) * scale + bias_ref[h, :, :NT]
        weight = jnp.exp(scores - jnp.max(scores, axis=-1, keepdims=True))
        prob = weight / jnp.sum(weight, axis=-1, keepdims=True)
        prob_ref[h, :, :NT] = prob
        mixed = mixed + mm(prob.astype(BF16), value * picks[h])
    mixture = mixed.astype(BF16)
    loads["proj"].wait()
    xs[1] = mm(mixture, wproj_ref[...]).astype(BF16)
    copies = send_slots(1, afters)

    cot = mm(grid, cot_ref[...]).astype(BF16)
    loads["down"].wait()
    delta_act = mm(cot, wdown_ref[...])
    buf1[2304:, :] = jnp.zeros((buf1.shape[0] - 2304, LANES), BF16)
    buf2[1152:, :] = jnp.zeros((buf2.shape[0] - 1152, LANES), BF16)
    bufb[...] = jnp.zeros(bufb.shape, BF16)
    ds_ref[...] = jnp.zeros(ds_ref.shape, F32)
    gains_lat[0] = jnp.zeros((8, 256), F32)
    loads["up"].wait()
    finish(copies)

    middle = (tokens + xr[1].astype(F32)).astype(BF16).astype(F32)
    normal_two, inverse_two = norm_stats(middle)
    gain_two = gain2_ref[...]
    normed_two = (normal_two * gain_two).astype(BF16)
    up = mm(normed_two, wup_ref[...])
    cumulative = 0.5 * (1.0 + lax.erf(up * 0.7071067811865476))
    density = jnp.exp(-0.5 * up * up) * 0.3989422804014327
    active = (up * cumulative).astype(BF16)
    delta_up = (delta_act * (cumulative + up * density)).astype(BF16)
    delta_hidden = mm_nt(delta_up, wup_ref[...])
    delta_input, grad_gain_two = norm_back(delta_hidden, normal_two, inverse_two, gain_two)
    delta_middle = (cot.astype(F32) + delta_input).astype(BF16)
    xs[2] = delta_middle
    copies = send_slots(2, befores)

    grad_up = mm_tn(normed_two, delta_up).astype(BF16)
    for j in range(6):
        buf1[j * C : (j + 1) * C, :] = grad_up[:, j * LANES : (j + 1) * LANES]
    grad_down = mm_tn(cot, active).astype(BF16)
    for j in range(6):
        buf1[(6 + j) * C : (7 + j) * C, :] = grad_down[:, j * LANES : (j + 1) * LANES]

    def exchange(axis, k):
        if axis == 0:
            return Exchange(place, 0, lat_send.at[k], lat_recv.at[k])
        return Exchange(place, 1, lon_send.at[k], lon_recv.at[k])

    rq1, rq2 = rp1 * n_lon, rp2 * n_lon
    scatter_lat1 = exchange(0, 0)
    scatter_lat1.scatter(buf1, got1, rq1)
    output = middle + mm_nt(active, wdown_ref[...])
    out_ref[...] = mm_tn(grid, output.astype(BF16)).astype(BF16)
    finish(copies)

    delta_attn = xr[2]
    delta_mix = mm_nt(delta_attn, wproj_ref[...]).astype(BF16)
    pack_ref[:, 3 * C :] = mm_tn(mixture, delta_attn)
    delta_query, delta_key, delta_value = (jnp.zeros((NT, C), F32) for _ in range(3))
    for h in range(HEADS):
        delta_head = delta_mix * picks[h]
        prob = prob_ref[h, :, :NT]
        delta_prob = mm_nt(delta_head, value)
        scored = prob * (delta_prob - jnp.sum(delta_prob * prob, axis=-1, keepdims=True))
        ds_ref[h, :, :NT] = scored
        low = scored.astype(BF16)
        delta_query = delta_query + mm(low, key * picks[h])
        delta_key = delta_key + mm_tn(low, query * picks[h])
        delta_value = delta_value + mm_tn(prob.astype(BF16), delta_head)
    delta_query = (delta_query * scale).astype(BF16)
    delta_key = (delta_key * scale).astype(BF16)
    delta_value = delta_value.astype(BF16)
    w_qkv = wqkv_ref[...]
    xs[3] = (
        mm_nt(delta_query, w_qkv[:, :C])
        + mm_nt(delta_key, w_qkv[:, C : 2 * C])
        + mm_nt(delta_value, w_qkv[:, 2 * C :])
    ).astype(BF16)
    copies = send_slots(3, afters)

    pack_ref[:, :C] = mm_tn(windows, delta_query)
    pack_ref[:, C : 2 * C] = mm_tn(windows, delta_key)
    pack_ref[:, 2 * C : 3 * C] = mm_tn(windows, delta_value)
    for j in range(6):
        buf2[j * C : (j + 1) * C, :] = pack_ref[:, j * LANES : (j + 1) * LANES].astype(BF16)
    scatter_lat2 = exchange(0, 1)
    scatter_lat2.scatter(buf2, got2, rq2)
    mid1[...] = scatter_lat1.total().astype(BF16)
    scatter_lon1 = exchange(1, 0)
    scatter_lon1.scatter(mid1, gom1, rp1)

    iota_hi = lax.broadcasted_iota(jnp.int32, (HI, 256), 0)
    iota_lo = lax.broadcasted_iota(jnp.int32, (LANES, 256), 0)

    def collect(block, acc):
        slot = block // 5
        rows = pl.ds(pl.multiple_of(slot * SLOT + (block - slot * 5) * 8, 8), 8)
        hi_rows, lo_rows = hi_ref[rows, :], lo_ref[rows, :]
        ds_rows = [ds_ref[h, rows, :] for h in range(HEADS)]
        left, right = [], []
        for i in range(8):
            here = iota_hi == hi_rows[i : i + 1, :]
            left.append(
                jnp.concatenate(
                    [jnp.where(here, rows_h[i : i + 1, :], 0.0).astype(BF16) for rows_h in ds_rows],
                    axis=0,
                )
            )
            right.append(
                jnp.where(iota_lo == lo_rows[i : i + 1, :], 1.0, 0.0).astype(BF16)
            )
        return acc + mm_nt(jnp.concatenate(left, axis=1), jnp.concatenate(right, axis=1))

    bias_sum = lax.fori_loop(0, 8, collect, jnp.zeros((HEADS * HI, LANES), F32))
    finish(copies)

    delta_normed = xr[3].astype(F32)
    delta_input, grad_gain_one = norm_back(delta_normed, normal_one, inverse_one, gain_one)
    gains_lat[0, 0:1, :C] = grad_gain_one
    gains_lat[0, 1:2, :C] = grad_gain_two
    gain_lat = exchange(0, 3)
    for d in range(1, n_lat):
        gain_lat.start(d, gains_lat.at[0], gains_lat.at[d], gain_lat.peer(d)[1])

    mid2[...] = scatter_lat2.total().astype(BF16)
    scatter_lon2 = exchange(1, 3)
    scatter_lon2.scatter(mid2, gom2, rp2)

    def own_rows(rows):
        return pl.multiple_of((lat * n_lon + lon) * rows, 16)

    start1 = own_rows(rp1)
    all1[pl.ds(start1, rp1), :] = (scatter_lon1.total() * factor).astype(BF16)
    gather_lon1 = exchange(1, 1)
    gather_lon1.gather(all1, rp1, start1)

    bias_sum = lax.fori_loop(8, 20, collect, bias_sum)
    bufb[: HEADS * HI, :] = bias_sum.astype(BF16)
    scatter_b = exchange(1, 2)
    scatter_b.scatter(bufb, gotb, rpb)

    start2 = own_rows(rp2)
    all2[pl.ds(start2, rp2), :] = (scatter_lon2.total() * factor).astype(BF16)
    gather_lon2 = exchange(1, 5)
    gather_lon2.gather(all2, rp2, start2)

    gain_lat.wait()
    gains_lon[0] = jnp.sum(gains_lat[...], axis=0)
    gain_lon = exchange(1, 6)
    for d in range(1, n_lon):
        gain_lon.start(d, gains_lon.at[0], gains_lon.at[d], gain_lon.peer(d)[1])

    gather_lon1.wait()
    gather_lat1 = exchange(0, 2)
    gather_lat1.gather(all1, rq1, pl.multiple_of(lat * rq1, 16))

    startb = pl.multiple_of(lon * rpb, 16)
    allb[pl.ds(startb, rpb), :] = scatter_b.total().astype(BF16)
    gather_b = exchange(1, 4)
    gather_b.gather(allb, rpb, startb)

    gather_lon2.wait()
    gather_lat2 = exchange(0, 4)
    gather_lat2.gather(all2, rq2, pl.multiple_of(lat * rq2, 16))

    delta_tokens = (delta_middle.astype(F32) + delta_input).astype(BF16)
    dtok_ref[...] = mm_tn(grid, delta_tokens).astype(BF16)
    gain_lon.wait()
    ggain_ref[...] = jnp.sum(gains_lon[...], axis=0) * factor
    gather_b.wait()
    gather_lat1.wait()
    gather_lat2.wait()


def unpack(
    ggain_in,
    all1,
    all2,
    allb,
    gain1_ref,
    gain2_ref,
    gqkv_ref,
    gproj_ref,
    gup_ref,
    gdown_ref,
    gbias_ref,
    pack_ref,
):
    gain1_ref[...] = ggain_in[0:1, :C]
    gain2_ref[...] = ggain_in[1:2, :C]
    for j in range(6):
        cols = slice(j * LANES, (j + 1) * LANES)
        gup_ref[:, cols] = all1[j * C : (j + 1) * C, :].astype(F32)
        gdown_ref[:, cols] = all1[(6 + j) * C : (7 + j) * C, :].astype(F32)
        pack_ref[:, cols] = all2[j * C : (j + 1) * C, :].astype(F32)
    gqkv_ref[...] = pack_ref[:, : 3 * C]
    gproj_ref[...] = pack_ref[:, 3 * C :]
    for h in range(HEADS):
        rows = allb[h * HI : (h + 1) * HI, :].astype(F32)
        for k in range(HI_USED):
            wide = min(LANES, NPOS - k * LANES)
            gbias_ref[h, :, k * LANES : k * LANES + wide] = rows[k : k + 1, :wide]


def up_to(value, unit):
    return -(-value // unit) * unit


def local(
    n_lat,
    n_lon,
    tokens,
    gain_one,
    gain_two,
    qkv_weight,
    proj_weight,
    up_weight,
    down_weight,
    bias_table,
    pos_index,
    mask_ids,
    cotangent,
):
    n = n_lat * n_lon
    factor = 1.0 / math.sqrt(WT * n)
    rp1 = up_to(-(-2304 // n), 16)
    rp2 = up_to(-(-1152 // n), 16)
    rpb = up_to(-(-HEADS * HI // n_lon), 16)
    grid, window = orders()
    args = (
        tokens.reshape(WT, C),
        cotangent.reshape(WT, C),
        gain_one.reshape(1, C),
        gain_two.reshape(1, C),
        qkv_weight,
        proj_weight,
        up_weight,
        down_weight.T,
        bias_table.reshape(HEADS, 1, NPOS),
        pos_index,
        mask_ids.reshape(1, WT),
        jnp.asarray(grid, BF16),
        jnp.asarray(window, BF16),
    )
    shape = jax.ShapeDtypeStruct
    outs = (
        shape((WT, C), BF16),
        shape((WT, C), BF16),
        shape((8, 256), F32),
        shape((rp1 * n, LANES), BF16),
        shape((rp2 * n, LANES), BF16),
        shape((rpb * n_lon, LANES), BF16),
    )

    def rows(count):
        return pltpu.VMEM((count, LANES), BF16)

    dma = pltpu.SemaphoreType.DMA
    scratch = [
        pltpu.VMEM((C, 3 * C), BF16),
        pltpu.VMEM((C, C), BF16),
        pltpu.VMEM((C, HID), BF16),
        pltpu.VMEM((C, HID), BF16),
        pltpu.VMEM((WT, WT), jnp.int32),
        pltpu.VMEM((256, WT), BF16),
        dma((6,)),
        pltpu.VMEM((HEADS * HI, LANES), F32),
        pltpu.VMEM((4, NT, C), BF16),
        pltpu.VMEM((4, NT, C), BF16),
        pltpu.VMEM((NT, 256), jnp.int32),
        pltpu.VMEM((NT, 256), jnp.int32),
        pltpu.VMEM((HEADS, NT, 256), F32),
        pltpu.VMEM((HEADS, NT, 256), F32),
        pltpu.VMEM((HEADS, NT, 256), F32),
        pltpu.VMEM((C, HID), F32),
        pltpu.VMEM((n_lat, 8, 256), F32),
        pltpu.VMEM((n_lon, 8, 256), F32),
    ]
    for rp in (rp1, rp2):
        scratch += [
            rows(rp * n),
            rows(rp * n_lon * (n_lat - 1)),
            rows(rp * n_lon),
            rows(rp * (n_lon - 1)),
        ]
    scratch += [rows(rpb * n_lon), rows(rpb * (n_lon - 1))]
    scratch += [
        dma((4, 3)),
        dma((4, 3)),
        dma((5, n_lat - 1)),
        dma((5, n_lat - 1)),
        dma((7, n_lon - 1)),
        dma((7, n_lon - 1)),
    ]
    vmem = pl.BlockSpec(memory_space=pltpu.VMEM)
    hbm = pl.BlockSpec(memory_space=pltpu.HBM)
    in_specs = [vmem] * 4 + [hbm] * 4 + [vmem, hbm, vmem, vmem, hbm]
    out, dtok, *sums = pl.pallas_call(
        functools.partial(kernel, n_lat, n_lon, factor, rp1, rp2, rpb),
        out_shape=outs,
        in_specs=in_specs,
        out_specs=[vmem] * len(outs),
        scratch_shapes=scratch,
        compiler_params=pltpu.CompilerParams(
            collective_id=0, has_side_effects=True, vmem_limit_bytes=48 * 1024 * 1024
        ),
    )(*args)
    results = (
        shape((1, C), F32),
        shape((1, C), F32),
        shape((C, 3 * C), F32),
        shape((C, C), F32),
        shape((C, HID), F32),
        shape((C, HID), F32),
        shape((HEADS, 1, NPOS), F32),
    )
    gain1, gain2, gqkv, gproj, gup, gdown, gbias = pl.pallas_call(
        unpack,
        out_shape=results,
        in_specs=[vmem] * len(sums),
        out_specs=[vmem] * len(results),
        scratch_shapes=[pltpu.VMEM((C, HID), F32)],
        compiler_params=pltpu.CompilerParams(vmem_limit_bytes=32 * 1024 * 1024),
    )(*sums)
    return (
        out.reshape(tokens.shape),
        dtok.reshape(tokens.shape),
        gain1.reshape(C),
        gain2.reshape(C),
        gqkv,
        gproj,
        gup,
        gdown.T,
        gbias.reshape(bias_table.shape),
    )


def solution(mesh):
    grid = P(None, "lat", "lon", None)
    table = P(None, None, "lat", None)
    in_specs = (grid, P(), P(), P(), P(), P(), P(), table, P(), P(None, "lat", "lon"), grid)
    out_specs = (grid, grid, P(), P(), P(), P(), P(), P(), table)
    body = functools.partial(local, mesh.shape["lat"], mesh.shape["lon"])
    return jax.shard_map(
        body, mesh=mesh, in_specs=in_specs, out_specs=out_specs, check_vma=False
    )
```

```python
import functools
import math

import jax
import jax.numpy as jnp
from jax import lax
from jax.experimental import pallas as pl
from jax.experimental.pallas import tpu as pltpu
from jax.sharding import PartitionSpec as P

HEADS = 6
WZ = 2
WLAT = 6
WLON = 12
WT = 144
NPOS = 3312
C = 192
HID = 768
HD = 32
SLOT = 48
NT = 4 * SLOT
LANES = 128
HI = 32
HI_USED = -(-NPOS // LANES)
EPS = 1e-05
F32 = jnp.float32
BF16 = jnp.bfloat16
MESH = pl.DeviceIdType.MESH


def order(rows, window):
    row = lax.broadcasted_iota(jnp.int32, (rows, 1), 0)
    slot = (row * 171) >> 13
    rest = row - slot * SLOT
    z = (rest * 57) >> 10
    inner = rest - z * 18
    r = (inner * 43) >> 8
    c = inner - r * 6
    rh, ch = slot >> 1, slot & 1
    if window:
        z, rh, ch = 1 - z, 1 - rh, 1 - ch
    token = z * 72 + (3 * rh + r) * 12 + 6 * ch + c
    token = jnp.where((rest < 36) & (slot < 4), token, -1)
    lane = lax.broadcasted_iota(jnp.int32, (rows, WT), 1)
    return jnp.where(lane == token, 1.0, 0.0).astype(BF16)


def mm(a, b):
    return lax.dot_general(a, b, (((1,), (0,)), ((), ())), preferred_element_type=F32)


def mm_nt(a, b):
    return lax.dot_general(a, b, (((1,), (1,)), ((), ())), preferred_element_type=F32)


def mm_tn(a, b):
    return lax.dot_general(a, b, (((0,), (0,)), ((), ())), preferred_element_type=F32)


def norm_stats(widened):
    center = widened - jnp.mean(widened, axis=-1, keepdims=True)
    spread = jnp.mean(center * center, axis=-1, keepdims=True)
    inverse = lax.rsqrt(spread + EPS)
    return center * inverse, inverse


def norm_back(delta_hidden, normal, inverse, gain):
    grad_gain = jnp.sum(delta_hidden * normal, axis=0, keepdims=True)
    delta_normal = delta_hidden * gain
    delta_input = inverse * (
        delta_normal
        - jnp.mean(delta_normal, axis=-1, keepdims=True)
        - normal * jnp.mean(delta_normal * normal, axis=-1, keepdims=True)
    )
    return delta_input, grad_gain


class Exchange:
    def __init__(self, place, axis, send_sem, recv_sem):
        self.lat, self.lon, self.n_lat, self.n_lon = place
        self.axis = axis
        self.n = self.n_lat if axis == 0 else self.n_lon
        self.me = self.lat if axis == 0 else self.lon
        self.send_sem, self.recv_sem = send_sem, recv_sem
        self.copies = []

    def peer(self, d):
        to = lax.rem(self.me + d, self.n)
        return to, ((to, self.lon) if self.axis == 0 else (self.lat, to))

    def start(self, d, src, dst, device):
        copy = pltpu.make_async_remote_copy(
            src_ref=src,
            dst_ref=dst,
            send_sem=self.send_sem.at[d - 1],
            recv_sem=self.recv_sem.at[d - 1],
            device_id=device,
            device_id_type=MESH,
        )
        copy.start()
        self.copies.append(copy)

    def scatter(self, src, got, rows):
        self.src, self.got, self.rows = src, got, rows
        for d in range(1, self.n):
            to, device = self.peer(d)
            piece = pl.ds(pl.multiple_of(to * rows, 16), rows)
            self.start(d, src.at[piece], got.at[pl.ds((d - 1) * rows, rows)], device)

    def gather(self, whole, rows, start):
        piece = pl.ds(start, rows)
        for d in range(1, self.n):
            _, device = self.peer(d)
            self.start(d, whole.at[piece], whole.at[piece], device)

    def wait(self):
        for copy in self.copies:
            copy.wait()

    def total(self):
        self.wait()
        rows = self.rows
        own = pl.ds(pl.multiple_of(self.me * rows, 16), rows)
        out = self.src[own, :].astype(F32)
        for d in range(1, self.n):
            out = out + self.got[pl.ds((d - 1) * rows, rows), :].astype(F32)
        return out


def kernel(
    n_lat,
    n_lon,
    factor,
    rp1,
    rp2,
    rpb,
    tokens_ref,
    cot_ref,
    gain1_ref,
    gain2_ref,
    wqkv_in,
    wproj_in,
    wup_in,
    wdown_in,
    table_in,
    pos_in,
    mask_ref,
    out_ref,
    dtok_ref,
    ggain_ref,
    all1,
    all2,
    allb,
    wqkv_ref,
    wproj_ref,
    wup_ref,
    wdown_ref,
    pos_ref,
    load_sem,
    table_ref,
    xs,
    xr,
    hi_ref,
    lo_ref,
    bias_ref,
    prob_ref,
    ds_ref,
    pack_ref,
    gains_lat,
    gains_lon,
    buf1,
    got1,
    mid1,
    gom1,
    buf2,
    got2,
    mid2,
    gom2,
    bufb,
    gotb,
    x_send,
    x_recv,
    lat_send,
    lat_recv,
    lon_send,
    lon_recv,
):
    lat, lon = lax.axis_index("lat"), lax.axis_index("lon")
    place = (lat, lon, n_lat, n_lon)
    next_lat, next_lon = lax.rem(lat + 1, n_lat), lax.rem(lon + 1, n_lon)
    prev_lat, prev_lon = lax.rem(lat + n_lat - 1, n_lat), lax.rem(lon + n_lon - 1, n_lon)
    befores = ((prev_lat, prev_lon), (prev_lat, lon), (lat, prev_lon))
    afters = ((next_lat, next_lon), (next_lat, lon), (lat, next_lon))

    barrier = pltpu.get_barrier_semaphore()
    peers = [(lax.rem(lat + d, n_lat), lon) for d in range(1, n_lat)]
    peers += [(lat, lax.rem(lon + d, n_lon)) for d in range(1, n_lon)]
    peers += [befores[0], afters[0]]
    for peer in peers:
        pl.semaphore_signal(barrier, inc=1, device_id=peer, device_id_type=MESH)

    loads = {}
    for k, (name, src, dst) in enumerate(
        (
            ("pos", pos_in, pos_ref),
            ("qkv", wqkv_in, wqkv_ref),
            ("proj", wproj_in, wproj_ref),
            ("down", wdown_in, wdown_ref),
            ("up", wup_in, wup_ref),
        )
    ):
        loads[name] = pltpu.make_async_copy(src, dst, load_sem.at[k])
        loads[name].start()

    def send_slots(e, devices):
        copies = []
        for s in range(3):
            piece = pl.ds(s * SLOT, SLOT)
            copy = pltpu.make_async_remote_copy(
                src_ref=xs.at[e, piece],
                dst_ref=xr.at[e, piece],
                send_sem=x_send.at[e, s],
                recv_sem=x_recv.at[e, s],
                device_id=devices[s],
                device_id_type=MESH,
            )
            copy.start()
            copies.append(copy)
        xr[e, 3 * SLOT :, :] = xs[e, 3 * SLOT :, :]
        return copies

    def finish(copies):
        for copy in copies:
            copy.wait()

    grid = order(NT, False)
    tokens = mm(grid, tokens_ref[...])
    normal_one, inverse_one = norm_stats(tokens)
    gain_one = gain1_ref[...]
    xs[0] = (normal_one * gain_one).astype(BF16)
    pl.semaphore_wait(barrier, len(peers))
    copies = send_slots(0, befores)

    loads["pos"].wait()
    for h in range(HEADS):
        for k in range(HI_USED):
            wide = min(LANES, NPOS - k * LANES)
            row = pl.ds(h * HI + k, 1)
            table_ref[row, :wide] = table_in[h, :, k * LANES : k * LANES + wide]
        if NPOS % LANES:
            table_ref[h * HI + HI_USED - 1 : h * HI + HI_USED, NPOS % LANES :] = jnp.zeros(
                (1, LANES - NPOS % LANES), F32
            )
    win = order(256, True)
    win_rows = win[:NT]
    pos = pos_ref[...]
    hi = (pos >> 7).astype(F32).astype(BF16)
    lo = (pos & 127).astype(F32).astype(BF16)
    hi_ref[...] = mm_nt(mm(win_rows, hi).astype(BF16), win).astype(jnp.int32)
    lo_ref[...] = mm_nt(mm(win_rows, lo).astype(BF16), win).astype(jnp.int32)
    mask = jnp.broadcast_to((mask_ref[...] + 1).astype(F32), (8, WT)).astype(BF16)
    mask_row = mm_nt(mask, win)[0:1, :]
    mask_col = mm_nt(win_rows, mask)[:, 0:1]
    prob_ref[0] = jnp.where(mask_col == mask_row, 0.0, -1e30)

    step = 16

    def pick(block, carry):
        rows = pl.ds(pl.multiple_of(block * step, step), step)
        for half in range(2):
            cols = pl.ds(half * LANES, LANES)
            hi_here, lo_here = hi_ref[rows, cols], lo_ref[rows, cols]
            drop = prob_ref[0, rows, cols]
            acc = [drop] * HEADS
            for k in range(HI_USED):
                here = hi_here == k
                for h in range(HEADS):
                    row = jnp.broadcast_to(table_ref[pl.ds(h * HI + k, 1), :], (step, LANES))
                    got = jnp.take_along_axis(row, lo_here, axis=1, mode="promise_in_bounds")
                    acc[h] = jnp.where(here, got + drop, acc[h])
            for h in range(HEADS):
                bias_ref[h, rows, cols] = acc[h]
        return carry

    lax.fori_loop(0, NT // step, pick, 0)

    finish(copies)
    windows = xr[0]
    loads["qkv"].wait()
    packed = mm(windows, wqkv_ref[...]).astype(BF16)
    query, key, value = (packed[:, part * C : (part + 1) * C] for part in range(3))
    scale = HD**-0.5
    lane_head = lax.broadcasted_iota(jnp.int32, (1, C), 1) // HD
    picks = [jnp.where(lane_head == h, 1.0, 0.0).astype(BF16) for h in range(HEADS)]

    mixed = jnp.zeros((NT, C), F32)
    for h in range(HEADS):
        scores = mm_nt(query * picks[h], key) * scale + bias_ref[h, :, :NT]
        weight = jnp.exp(scores - jnp.max(scores, axis=-1, keepdims=True))
        prob = weight / jnp.sum(weight, axis=-1, keepdims=True)
        prob_ref[h, :, :NT] = prob
        mixed = mixed + mm(prob.astype(BF16), value * picks[h])
    mixture = mixed.astype(BF16)
    loads["proj"].wait()
    xs[1] = mm(mixture, wproj_ref[...]).astype(BF16)
    copies = send_slots(1, afters)

    cot = mm(grid, cot_ref[...]).astype(BF16)
    loads["down"].wait()
    delta_act = mm(cot, wdown_ref[...])
    buf1[2304:, :] = jnp.zeros((buf1.shape[0] - 2304, LANES), BF16)
    buf2[1152:, :] = jnp.zeros((buf2.shape[0] - 1152, LANES), BF16)
    bufb[...] = jnp.zeros(bufb.shape, BF16)
    ds_ref[...] = jnp.zeros(ds_ref.shape, F32)
    gains_lat[0] = jnp.zeros((8, 256), F32)
    loads["up"].wait()
    finish(copies)

    middle = (tokens + xr[1].astype(F32)).astype(BF16).astype(F32)
    normal_two, inverse_two = norm_stats(middle)
    gain_two = gain2_ref[...]
    normed_two = (normal_two * gain_two).astype(BF16)
    up = mm(normed_two, wup_ref[...])
    cumulative = 0.5 * (1.0 + lax.erf(up * 0.7071067811865476))
    density = jnp.exp(-0.5 * up * up) * 0.3989422804014327
    active = (up * cumulative).astype(BF16)
    delta_up = (delta_act * (cumulative + up * density)).astype(BF16)
    delta_hidden = mm_nt(delta_up, wup_ref[...])
    delta_input, grad_gain_two = norm_back(delta_hidden, normal_two, inverse_two, gain_two)
    delta_middle = (cot.astype(F32) + delta_input).astype(BF16)
    xs[2] = delta_middle
    copies = send_slots(2, befores)

    grad_up = mm_tn(normed_two, delta_up).astype(BF16)
    for j in range(6):
        buf1[j * C : (j + 1) * C, :] = grad_up[:, j * LANES : (j + 1) * LANES]
    grad_down = mm_tn(cot, active).astype(BF16)
    for j in range(6):
        buf1[(6 + j) * C : (7 + j) * C, :] = grad_down[:, j * LANES : (j + 1) * LANES]

    def exchange(axis, k):
        if axis == 0:
            return Exchange(place, 0, lat_send.at[k], lat_recv.at[k])
        return Exchange(place, 1, lon_send.at[k], lon_recv.at[k])

    rq1, rq2 = rp1 * n_lon, rp2 * n_lon
    scatter_lat1 = exchange(0, 0)
    scatter_lat1.scatter(buf1, got1, rq1)
    output = middle + mm_nt(active, wdown_ref[...])
    out_ref[...] = mm_tn(grid, output.astype(BF16)).astype(BF16)
    finish(copies)

    delta_attn = xr[2]
    delta_mix = mm_nt(delta_attn, wproj_ref[...]).astype(BF16)
    pack_ref[:, 3 * C :] = mm_tn(mixture, delta_attn)
    delta_query, delta_key, delta_value = (jnp.zeros((NT, C), F32) for _ in range(3))
    for h in range(HEADS):
        delta_head = delta_mix * picks[h]
        prob = prob_ref[h, :, :NT]
        delta_prob = mm_nt(delta_head, value)
        scored = prob * (delta_prob - jnp.sum(delta_prob * prob, axis=-1, keepdims=True))
        ds_ref[h, :, :NT] = scored
        low = scored.astype(BF16)
        delta_query = delta_query + mm(low, key * picks[h])
        delta_key = delta_key + mm_tn(low, query * picks[h])
        delta_value = delta_value + mm_tn(prob.astype(BF16), delta_head)
    delta_query = (delta_query * scale).astype(BF16)
    delta_key = (delta_key * scale).astype(BF16)
    delta_value = delta_value.astype(BF16)
    w_qkv = wqkv_ref[...]
    xs[3] = (
        mm_nt(delta_query, w_qkv[:, :C])
        + mm_nt(delta_key, w_qkv[:, C : 2 * C])
        + mm_nt(delta_value, w_qkv[:, 2 * C :])
    ).astype(BF16)
    copies = send_slots(3, afters)

    pack_ref[:, :C] = mm_tn(windows, delta_query)
    pack_ref[:, C : 2 * C] = mm_tn(windows, delta_key)
    pack_ref[:, 2 * C : 3 * C] = mm_tn(windows, delta_value)
    for j in range(6):
        buf2[j * C : (j + 1) * C, :] = pack_ref[:, j * LANES : (j + 1) * LANES].astype(BF16)
    scatter_lat2 = exchange(0, 1)
    scatter_lat2.scatter(buf2, got2, rq2)
    mid1[...] = scatter_lat1.total().astype(BF16)
    scatter_lon1 = exchange(1, 0)
    scatter_lon1.scatter(mid1, gom1, rp1)

    iota_hi = lax.broadcasted_iota(jnp.int32, (HI, 256), 0)
    iota_lo = lax.broadcasted_iota(jnp.int32, (LANES, 256), 0)

    def collect(block, acc):
        slot = block // 5
        rows = pl.ds(pl.multiple_of(slot * SLOT + (block - slot * 5) * 8, 8), 8)
        hi_rows, lo_rows = hi_ref[rows, :], lo_ref[rows, :]
        ds_rows = [ds_ref[h, rows, :] for h in range(HEADS)]
        left, right = [], []
        for i in range(8):
            here = iota_hi == hi_rows[i : i + 1, :]
            left.append(
                jnp.concatenate(
                    [jnp.where(here, rows_h[i : i + 1, :], 0.0).astype(BF16) for rows_h in ds_rows],
                    axis=0,
                )
            )
            right.append(
                jnp.where(iota_lo == lo_rows[i : i + 1, :], 1.0, 0.0).astype(BF16)
            )
        return acc + mm_nt(jnp.concatenate(left, axis=1), jnp.concatenate(right, axis=1))

    bias_sum = lax.fori_loop(0, 8, collect, jnp.zeros((HEADS * HI, LANES), F32))
    finish(copies)

    delta_normed = xr[3].astype(F32)
    delta_input, grad_gain_one = norm_back(delta_normed, normal_one, inverse_one, gain_one)
    gains_lat[0, 0:1, :C] = grad_gain_one
    gains_lat[0, 1:2, :C] = grad_gain_two
    gain_lat = exchange(0, 3)
    for d in range(1, n_lat):
        gain_lat.start(d, gains_lat.at[0], gains_lat.at[d], gain_lat.peer(d)[1])

    mid2[...] = scatter_lat2.total().astype(BF16)
    scatter_lon2 = exchange(1, 3)
    scatter_lon2.scatter(mid2, gom2, rp2)

    def own_rows(rows):
        return pl.multiple_of((lat * n_lon + lon) * rows, 16)

    start1 = own_rows(rp1)
    all1[pl.ds(start1, rp1), :] = (scatter_lon1.total() * factor).astype(BF16)
    gather_lon1 = exchange(1, 1)
    gather_lon1.gather(all1, rp1, start1)

    bias_sum = lax.fori_loop(8, 20, collect, bias_sum)
    bufb[: HEADS * HI, :] = bias_sum.astype(BF16)
    scatter_b = exchange(1, 2)
    scatter_b.scatter(bufb, gotb, rpb)

    start2 = own_rows(rp2)
    all2[pl.ds(start2, rp2), :] = (scatter_lon2.total() * factor).astype(BF16)
    gather_lon2 = exchange(1, 5)
    gather_lon2.gather(all2, rp2, start2)

    gain_lat.wait()
    gains_lon[0] = jnp.sum(gains_lat[...], axis=0)
    gain_lon = exchange(1, 6)
    for d in range(1, n_lon):
        gain_lon.start(d, gains_lon.at[0], gains_lon.at[d], gain_lon.peer(d)[1])

    gather_lon1.wait()
    gather_lat1 = exchange(0, 2)
    gather_lat1.gather(all1, rq1, pl.multiple_of(lat * rq1, 16))

    startb = pl.multiple_of(lon * rpb, 16)
    allb[pl.ds(startb, rpb), :] = scatter_b.total().astype(BF16)
    gather_b = exchange(1, 4)
    gather_b.gather(allb, rpb, startb)

    gather_lon2.wait()
    gather_lat2 = exchange(0, 4)
    gather_lat2.gather(all2, rq2, pl.multiple_of(lat * rq2, 16))

    delta_tokens = (delta_middle.astype(F32) + delta_input).astype(BF16)
    dtok_ref[...] = mm_tn(grid, delta_tokens).astype(BF16)
    gain_lon.wait()
    ggain_ref[...] = jnp.sum(gains_lon[...], axis=0) * factor
    gather_b.wait()
    gather_lat1.wait()
    gather_lat2.wait()


def unpack(
    ggain_in,
    all1,
    all2,
    allb,
    gain1_ref,
    gain2_ref,
    gqkv_ref,
    gproj_ref,
    gup_ref,
    gdown_ref,
    gbias_ref,
    pack_ref,
):
    gain1_ref[...] = ggain_in[0:1, :C]
    gain2_ref[...] = ggain_in[1:2, :C]
    for j in range(6):
        cols = slice(j * LANES, (j + 1) * LANES)
        gup_ref[:, cols] = all1[j * C : (j + 1) * C, :].astype(F32)
        gdown_ref[:, cols] = all1[(6 + j) * C : (7 + j) * C, :].astype(F32)
        pack_ref[:, cols] = all2[j * C : (j + 1) * C, :].astype(F32)
    gqkv_ref[...] = pack_ref[:, : 3 * C]
    gproj_ref[...] = pack_ref[:, 3 * C :]
    for h in range(HEADS):
        rows = allb[h * HI : (h + 1) * HI, :].astype(F32)
        for k in range(HI_USED):
            wide = min(LANES, NPOS - k * LANES)
            gbias_ref[h, :, k * LANES : k * LANES + wide] = rows[k : k + 1, :wide]


def up_to(value, unit):
    return -(-value // unit) * unit


def local(
    n_lat,
    n_lon,
    tokens,
    gain_one,
    gain_two,
    qkv_weight,
    proj_weight,
    up_weight,
    down_weight,
    bias_table,
    pos_index,
    mask_ids,
    cotangent,
):
    n = n_lat * n_lon
    factor = 1.0 / math.sqrt(WT * n)
    rp1 = up_to(-(-2304 // n), 16)
    rp2 = up_to(-(-1152 // n), 16)
    rpb = up_to(-(-HEADS * HI // n_lon), 16)
    args = (
        tokens.reshape(WT, C),
        cotangent.reshape(WT, C),
        gain_one.reshape(1, C),
        gain_two.reshape(1, C),
        qkv_weight,
        proj_weight,
        up_weight,
        down_weight.T,
        bias_table.reshape(HEADS, 1, NPOS),
        pos_index,
        mask_ids.reshape(1, WT),
    )
    shape = jax.ShapeDtypeStruct
    outs = (
        shape((WT, C), BF16),
        shape((WT, C), BF16),
        shape((8, 256), F32),
        shape((rp1 * n, LANES), BF16),
        shape((rp2 * n, LANES), BF16),
        shape((rpb * n_lon, LANES), BF16),
    )

    def rows(count):
        return pltpu.VMEM((count, LANES), BF16)

    dma = pltpu.SemaphoreType.DMA
    scratch = [
        pltpu.VMEM((C, 3 * C), BF16),
        pltpu.VMEM((C, C), BF16),
        pltpu.VMEM((C, HID), BF16),
        pltpu.VMEM((C, HID), BF16),
        pltpu.VMEM((WT, WT), jnp.int32),
        dma((5,)),
        pltpu.VMEM((HEADS * HI, LANES), F32),
        pltpu.VMEM((4, NT, C), BF16),
        pltpu.VMEM((4, NT, C), BF16),
        pltpu.VMEM((NT, 256), jnp.int32),
        pltpu.VMEM((NT, 256), jnp.int32),
        pltpu.VMEM((HEADS, NT, 256), F32),
        pltpu.VMEM((HEADS, NT, 256), F32),
        pltpu.VMEM((HEADS, NT, 256), F32),
        pltpu.VMEM((C, HID), F32),
        pltpu.VMEM((n_lat, 8, 256), F32),
        pltpu.VMEM((n_lon, 8, 256), F32),
    ]
    for rp in (rp1, rp2):
        scratch += [
            rows(rp * n),
            rows(rp * n_lon * (n_lat - 1)),
            rows(rp * n_lon),
            rows(rp * (n_lon - 1)),
        ]
    scratch += [rows(rpb * n_lon), rows(rpb * (n_lon - 1))]
    scratch += [
        dma((4, 3)),
        dma((4, 3)),
        dma((5, n_lat - 1)),
        dma((5, n_lat - 1)),
        dma((7, n_lon - 1)),
        dma((7, n_lon - 1)),
    ]
    vmem = pl.BlockSpec(memory_space=pltpu.VMEM)
    hbm = pl.BlockSpec(memory_space=pltpu.HBM)
    in_specs = [vmem] * 4 + [hbm] * 4 + [vmem, hbm, vmem]
    out, dtok, *sums = pl.pallas_call(
        functools.partial(kernel, n_lat, n_lon, factor, rp1, rp2, rpb),
        out_shape=outs,
        in_specs=in_specs,
        out_specs=[vmem] * len(outs),
        scratch_shapes=scratch,
        compiler_params=pltpu.CompilerParams(
            collective_id=0, has_side_effects=True, vmem_limit_bytes=48 * 1024 * 1024
        ),
    )(*args)
    results = (
        shape((1, C), F32),
        shape((1, C), F32),
        shape((C, 3 * C), F32),
        shape((C, C), F32),
        shape((C, HID), F32),
        shape((C, HID), F32),
        shape((HEADS, 1, NPOS), F32),
    )
    gain1, gain2, gqkv, gproj, gup, gdown, gbias = pl.pallas_call(
        unpack,
        out_shape=results,
        in_specs=[vmem] * len(sums),
        out_specs=[vmem] * len(results),
        scratch_shapes=[pltpu.VMEM((C, HID), F32)],
        compiler_params=pltpu.CompilerParams(vmem_limit_bytes=32 * 1024 * 1024),
    )(*sums)
    return (
        out.reshape(tokens.shape),
        dtok.reshape(tokens.shape),
        gain1.reshape(C),
        gain2.reshape(C),
        gqkv,
        gproj,
        gup,
        gdown.T,
        gbias.reshape(bias_table.shape),
    )


def solution(mesh):
    grid = P(None, "lat", "lon", None)
    table = P(None, None, "lat", None)
    in_specs = (grid, P(), P(), P(), P(), P(), P(), table, P(), P(None, "lat", "lon"), grid)
    out_specs = (grid, grid, P(), P(), P(), P(), P(), P(), table)
    body = functools.partial(local, mesh.shape["lat"], mesh.shape["lon"])
    return jax.shard_map(
        body, mesh=mesh, in_specs=in_specs, out_specs=out_specs, check_vma=False
    )
```
